32 devices in a mesh: row: 4 (over x, core), col: 8 (over z, y).
Axes of the slice: x: 2, y: 2, z: 4, core: 2. Of those that a mesh axis runs over, the one named last changes fastest.
Arguments:
- gradient: bfloat16 [6144, 24576], P('row', 'col'), may hold values from -60 to 60
Outputs:
- update: bfloat16 [6144, 24576], P('row', 'col')
The draws below stay inside these ranges and needn't reach their ends.
All inputs are finite; a program needn't handle non-finite values.
Results may differ from the reference program's by a relative error of at most 0.001.
The reference program's roundings to bfloat16 on the way count: a program that leaves them out, or rounds other values in their place, can miss the bound.
Values may be sent and summed in bfloat16 or wider, within the bound.
A program may use at most 128 MiB of HBM per device.

```python
import jax
import jax.numpy as jnp
from jax import lax

M = 6144
N = 24576
BLOCK = 1536


left_groups = 256


right_groups = 128


def draw_gradient(key, part):
    key = jax.random.fold_in(key, 7)
    keys = jax.random.split(key, 11)
    col_blocks = N // BLOCK
    rising = 3.0 ** (jnp.arange(M, dtype=jnp.float32) % BLOCK / BLOCK)
    column_group = jax.random.randint(keys[6], (N,), 0, left_groups)
    row_group = jax.random.randint(keys[7], (M,), 0, right_groups)
    values = jax.random.normal(keys[0], (M, N), jnp.float32)
    values = jnp.clip(values, -4.5, 4.5)
    row_scale = jnp.exp(jax.random.uniform(keys[1], (M, 1), jnp.float32, jnp.log(0.3), jnp.log(1.0)))
    mix_left = jnp.clip(jax.random.normal(keys[8], (M, left_groups), jnp.float32), -4.0, 4.0)
    mix_right = jnp.clip(jax.random.normal(keys[9], (right_groups, N), jnp.float32), -4.0, 4.0)
    row_scale = row_scale * rising[:, None]
    col_scale = jnp.exp(jax.random.uniform(keys[2], (1, N), jnp.float32, jnp.log(0.3), jnp.log(3.0)))
    left_vectors = jnp.clip(jax.random.normal(keys[4], (M, col_blocks), jnp.float32), -3.0, 3.0)
    right_vector = jnp.clip(jax.random.normal(keys[5], (1, N), jnp.float32), -3.0, 3.0)
    amplitude = 0.6 * 2.7 ** (jnp.arange(col_blocks, dtype=jnp.float32) / max(col_blocks - 1, 1))
    spread_left = jnp.repeat(left_vectors * amplitude[None, :], BLOCK, axis=1)
    spike = spread_left * right_vector
    col_weight = jnp.exp(jax.random.uniform(keys[10], (1, N), jnp.float32, jnp.log(0.5), jnp.log(2.0)))
    dense_left = jnp.take(mix_left, column_group, axis=1) * col_weight
    dense_right = jnp.take(mix_right, row_group, axis=0)
    mixed = values * row_scale * col_scale + spike + row_scale * (1.2 * dense_left + 0.8 * dense_right)
    return jnp.clip(mixed, -59.0, 59.0).astype(jnp.bfloat16)


def setup_inputs(seed: int = 0) -> dict:
    key_list = jax.random.split(jax.random.key(seed), 2)
    return {
        "gradient": draw_gradient(jax.random.fold_in(key_list[1], 71), 0),
    }


damping = 0.001

def root_of(gram):
    scale_value = jnp.sqrt(jnp.sum(gram * gram))
    identity = jnp.eye(BLOCK, dtype=jnp.float32)
    return ((5.0 * identity - gram / scale_value) * 0.25 * scale_value ** (-0.25)).astype(jnp.bfloat16)

def reference(gradient):
    rows_blocks = M // BLOCK
    cols_blocks = N // BLOCK
    identity = jnp.eye(BLOCK, dtype=jnp.float32)
    bands = gradient.reshape(rows_blocks, BLOCK, N)

    def left_block(band):
        gram = lax.dot_general(band, band, (((1,), (1,)), ((), ())), preferred_element_type=jnp.float32)
        return root_of(gram + damping * identity)
    left_roots = lax.map(left_block, bands)
    left_wide = left_roots.astype(jnp.float32)
    stripes = jnp.transpose(gradient.reshape(M, cols_blocks, BLOCK), (1, 0, 2))

    def column_block(stripe):
        gram = lax.dot_general(stripe, stripe, (((0,), (0,)), ((), ())), preferred_element_type=jnp.float32)
        right_root = root_of(gram + damping * identity)
        projected = jnp.dot(stripe, right_root, preferred_element_type=jnp.float32).astype(jnp.bfloat16)
        tiles = projected.reshape(rows_blocks, BLOCK, BLOCK).astype(jnp.float32)
        precond = jnp.einsum('ikl,ild->ikd', left_wide, tiles, precision=lax.Precision.HIGHEST)
        grad_tiles = stripe.reshape(rows_blocks, BLOCK, BLOCK).astype(jnp.float32)
        grad_sq = lax.optimization_barrier(jnp.sum(grad_tiles * grad_tiles, axis=(1, 2)))
        pre_sq = lax.optimization_barrier(jnp.sum(precond * precond, axis=(1, 2)))
        factor = jnp.sqrt(grad_sq) / jnp.sqrt(pre_sq + 1e-06)
        return (precond * factor[:, None, None]).astype(jnp.bfloat16)
    result = lax.map(column_block, stripes)
    return jnp.transpose(result, (1, 2, 0, 3)).reshape(M, N)
```

```python
import jax
import jax.numpy as jnp
from jax import lax
from jax.experimental import pallas as pl
from jax.experimental.pallas import tpu as pltpu
from jax.sharding import PartitionSpec as P

M = 6144
BLOCK = 1536
SUB = 256


damping = 0.001

STRIPS = BLOCK // SUB
PAIRS = [(a, b) for a in range(STRIPS) for b in range(a, STRIPS)]
SLOT = {pair: index for index, pair in enumerate(PAIRS)}
TRI = len(PAIRS)


def swapped(block, axis, apart):
    count = lax.axis_size(axis)
    route = []
    for low in range(count):
        high = low | 1 << apart
        if high != low and high < count:
            route += [(low, high), (high, low)]
    return lax.ppermute(block, axis, route)


def general(gradient):
    rows_dev, cols_dev = gradient.shape
    col_blocks = cols_dev // BLOCK
    share_count = BLOCK // rows_dev
    sections = share_count.bit_length() - 1
    row_count = lax.axis_size("row")
    row_index = lax.axis_index("row")
    row_blocks = M // BLOCK
    my_block = row_index // share_count
    offset = row_index % share_count * rows_dev
    slots = (jnp.arange(row_blocks) == my_block).astype(jnp.float32)
    band = gradient
    for bit in range(sections):
        partner = swapped(band, "row", bit)
        upper = row_index // 2**bit % 2 == 1
        band = jnp.where(
            upper, jnp.concatenate([partner, band], 0), jnp.concatenate([band, partner], 0)
        )
    grad_three = gradient.reshape(rows_dev, col_blocks, BLOCK)
    grad_wide = grad_three.astype(jnp.float32)
    grad_tiles = jnp.sum(grad_wide * grad_wide, axis=(0, 2))
    grad_slots = slots[:, None] * grad_tiles[None, :]
    grad_total = lax.psum(grad_slots, "row")
    left_part = lax.dot_general(
        gradient, band, (((1,), (1,)), ((), ())), preferred_element_type=jnp.float32
    )
    row_place = offset + lax.broadcasted_iota(jnp.int32, (rows_dev, 1), 0)
    left_rows = lax.psum(left_part, "col")
    diagonal = (lax.broadcasted_iota(jnp.int32, (rows_dev, BLOCK), 1) == row_place).astype(
        jnp.float32
    )
    left_rows = left_rows + damping * diagonal
    left_total = lax.psum(slots * jnp.sum(left_rows * left_rows), "row")
    left_scale = jnp.sqrt(jnp.sum(left_total * slots))
    left_root = ((5.0 * diagonal - left_rows / left_scale) * 0.25 * left_scale ** (-0.25)).astype(
        jnp.bfloat16
    )
    right_rows = BLOCK // row_count
    portion = grad_three
    right_share = lax.psum_scatter(
        jnp.einsum("rjc,rjd->cjd", portion, grad_three, preferred_element_type=jnp.float32),
        "row",
        scatter_dimension=0,
        tiled=True,
    )
    right_place = row_index * right_rows + lax.broadcasted_iota(
        jnp.int32, (right_rows, 1, BLOCK), 0
    )
    right_diagonal = (
        lax.broadcasted_iota(jnp.int32, (right_rows, 1, BLOCK), 2) == right_place
    ).astype(jnp.float32)
    right_share = right_share + damping * right_diagonal
    right_squares = jnp.sum(right_share * right_share, axis=(0, 2))
    right_total = lax.psum(right_squares, "row")
    right_scale = jnp.sqrt(right_total)[None, :, None]
    right_piece = (
        (5.0 * right_diagonal - right_share / right_scale) * 0.25 * right_scale ** (-0.25)
    ).astype(jnp.bfloat16)
    portion = grad_three
    projected = jnp.einsum(
        "rjc,cjd->rjd",
        portion,
        lax.all_gather(right_piece, "row", axis=0, tiled=True),
        preferred_element_type=jnp.float32,
    ).astype(jnp.bfloat16)
    projected_band = projected
    for bit in range(sections):
        partner_rows = swapped(projected_band, "row", bit)
        upper = row_index // 2**bit % 2 == 1
        projected_band = jnp.where(
            upper,
            jnp.concatenate([partner_rows, projected_band], 0),
            jnp.concatenate([projected_band, partner_rows], 0),
        )
    precond = jnp.einsum(
        "rk,kjd->rjd", left_root, projected_band, preferred_element_type=jnp.float32
    )
    pre_tiles = jnp.sum(precond * precond, axis=(0, 2))
    update_total = lax.psum(slots[:, None] * pre_tiles[None, :], "row")
    grad_mine = jnp.sum(grad_total * slots[:, None], axis=0)
    update_mine = jnp.sum(update_total * slots[:, None], axis=0)
    factor = jnp.sqrt(grad_mine) / jnp.sqrt(update_mine + 1e-06)
    return (precond * factor[None, :, None]).astype(jnp.bfloat16).reshape(rows_dev, cols_dev)


def eye():
    shape = (SUB, SUB)
    return lax.broadcasted_iota(jnp.int32, shape, 0) == lax.broadcasted_iota(jnp.int32, shape, 1)


def store_strip(a, strip, tri_ref, diag_ref):
    for b in range(a, STRIPS):
        block = strip[:, (b - a) * SUB : (b - a + 1) * SUB]
        if a == b:
            diag_ref[:, a * SUB : (a + 1) * SUB] = jnp.sum(
                jnp.where(eye(), block, 0.0), axis=0, keepdims=True
            )
        tri_ref[SLOT[a, b]] = block.astype(jnp.bfloat16)


def left_gram_kernel(g_ref, tri_ref, diag_ref):
    for a in range(STRIPS):
        strip = lax.dot_general(
            g_ref[a * SUB : (a + 1) * SUB, :],
            g_ref[a * SUB :, :],
            (((1,), (1,)), ((), ())),
            preferred_element_type=jnp.float32,
        )
        store_strip(a, strip, tri_ref, diag_ref)


def right_gram_kernel(g_ref, tri_ref, diag_ref):
    for a in range(STRIPS):
        strip = lax.dot_general(
            g_ref[:, a * SUB : (a + 1) * SUB],
            g_ref[:, a * SUB :],
            (((0,), (0,)), ((), ())),
            preferred_element_type=jnp.float32,
        )
        store_strip(a, strip, tri_ref, diag_ref)


def build_root(tri_ref, diag_ref, root_ref):
    diag = diag_ref[...] + damping
    total = jnp.sum(diag * diag, axis=1, keepdims=True)
    squares = jnp.zeros((SUB, SUB), jnp.float32)
    for a, b in PAIRS:
        block = tri_ref[SLOT[a, b]].astype(jnp.float32)
        if a == b:
            block = jnp.where(eye(), 0.0, block)
            squares = squares + block * block
        else:
            squares = squares + 2.0 * (block * block)
    squares = jnp.sum(jnp.sum(squares, axis=0, keepdims=True), axis=1, keepdims=True)
    scale = jnp.sqrt(total + squares)
    inverse = 1.0 / scale
    gain = 0.25 / jnp.sqrt(jnp.sqrt(scale))
    on_diag = (5.0 - diag * inverse) * gain
    for a, b in PAIRS:
        block = (0.0 - tri_ref[SLOT[a, b]].astype(jnp.float32) * inverse) * gain
        rows, cols = slice(a * SUB, (a + 1) * SUB), slice(b * SUB, (b + 1) * SUB)
        if a == b:
            block = jnp.where(eye(), on_diag[:, cols], block)
        else:
            root_ref[cols, rows] = block.T.astype(jnp.bfloat16)
        root_ref[rows, cols] = block.astype(jnp.bfloat16)


CHUNK = 512


def apply_kernel(
    g_ref, left_ref, left_diag, right_ref, right_diag, out_ref, left_root, right_root, proj, pre
):
    @pl.when(pl.program_id(0) == 0)
    def _():
        build_root(left_ref, left_diag, left_root)

    build_root(right_ref.at[0], right_diag, right_root)
    zero = jnp.zeros((8, CHUNK), jnp.float32)

    def sums(wide):
        return jnp.sum((wide * wide).reshape(-1, 8, CHUNK), axis=0)

    def step(n, carry):
        grad_sum, pre_sum = carry
        cols = pl.ds(pl.multiple_of(n * CHUNK, CHUNK), CHUNK)
        proj[...] = jnp.dot(
            g_ref[...], right_root[:, cols], preferred_element_type=jnp.float32
        ).astype(jnp.bfloat16)
        block = jnp.dot(left_root[...], proj[...], preferred_element_type=jnp.float32)
        pre[:, cols] = block
        return grad_sum + sums(g_ref[:, cols].astype(jnp.float32)), pre_sum + sums(block)

    grad_sum, pre_sum = lax.fori_loop(0, BLOCK // CHUNK, step, (zero, zero))

    def whole(part):
        return jnp.sum(jnp.sum(part, axis=0, keepdims=True), axis=1, keepdims=True)

    factor = jnp.sqrt(whole(grad_sum)) / jnp.sqrt(whole(pre_sum) + 1e-06)

    def scale_rows(m, carry):
        rows = pl.ds(pl.multiple_of(m * SUB, SUB), SUB)
        out_ref[rows, :] = (pre[rows, :] * factor).astype(jnp.bfloat16)
        return carry

    lax.fori_loop(0, STRIPS, scale_rows, 0)


VMEM_LIMIT = 60 * 1024 * 1024


def local(gradient):
    rows_dev, cols_dev = gradient.shape
    if rows_dev != BLOCK:
        return general(gradient)
    col_blocks = cols_dev // BLOCK
    params = pltpu.CompilerParams(vmem_limit_bytes=VMEM_LIMIT)
    flops = BLOCK * BLOCK * cols_dev
    left_tri, left_diag = pl.pallas_call(
        left_gram_kernel,
        out_shape=(
            jax.ShapeDtypeStruct((TRI, SUB, SUB), jnp.bfloat16),
            jax.ShapeDtypeStruct((1, BLOCK), jnp.float32),
        ),
        compiler_params=params,
        cost_estimate=pl.CostEstimate(flops=flops, bytes_accessed=13_000_000, transcendentals=0),
    )(gradient)
    left_tri = lax.psum(left_tri, "col")
    left_diag = lax.psum(left_diag, "col")
    right_tri, right_diag = pl.pallas_call(
        right_gram_kernel,
        grid=(col_blocks,),
        in_specs=[pl.BlockSpec((BLOCK, BLOCK), lambda j: (0, j))],
        out_specs=(
            pl.BlockSpec((None, TRI, SUB, SUB), lambda j: (j, 0, 0, 0)),
            pl.BlockSpec((1, BLOCK), lambda j: (0, j)),
        ),
        out_shape=(
            jax.ShapeDtypeStruct((col_blocks, TRI, SUB, SUB), jnp.bfloat16),
            jax.ShapeDtypeStruct((1, cols_dev), jnp.float32),
        ),
        compiler_params=params,
        cost_estimate=pl.CostEstimate(flops=flops, bytes_accessed=16_000_000, transcendentals=0),
    )(gradient)
    right_tri = lax.psum(right_tri, "row")
    right_diag = lax.psum(right_diag, "row")
    return pl.pallas_call(
        apply_kernel,
        grid=(col_blocks,),
        in_specs=[
            pl.BlockSpec((BLOCK, BLOCK), lambda j: (0, j)),
            pl.BlockSpec((TRI, SUB, SUB), lambda j: (0, 0, 0)),
            pl.BlockSpec((1, BLOCK), lambda j: (0, 0)),
            pl.BlockSpec((1, TRI, SUB, SUB), lambda j: (j, 0, 0, 0)),
            pl.BlockSpec((1, BLOCK), lambda j: (0, j)),
        ],
        out_specs=pl.BlockSpec((BLOCK, BLOCK), lambda j: (0, j)),
        out_shape=jax.ShapeDtypeStruct((BLOCK, cols_dev), jnp.bfloat16),
        scratch_shapes=[
            pltpu.VMEM((BLOCK, BLOCK), jnp.bfloat16),
            pltpu.VMEM((BLOCK, BLOCK), jnp.bfloat16),
            pltpu.VMEM((BLOCK, CHUNK), jnp.bfloat16),
            pltpu.VMEM((BLOCK, BLOCK), jnp.float32),
        ],
        compiler_params=params,
    )(gradient, left_tri, left_diag, right_tri, right_diag)


def solution(mesh):
    in_specs = (P("row", "col"),)
    out_specs = P("row", "col")
    return jax.shard_map(local, mesh=mesh, in_specs=in_specs, out_specs=out_specs, check_vma=False)
```

```python
import jax
import jax.numpy as jnp
from jax import lax
from jax.experimental import pallas as pl
from jax.experimental.pallas import tpu as pltpu
from jax.sharding import PartitionSpec as P

M = 6144
BLOCK = 1536
SUB = 256


damping = 0.001

STRIPS = BLOCK // SUB
PAIRS = [(a, b) for a in range(STRIPS) for b in range(a, STRIPS)]
SLOT = {pair: index for index, pair in enumerate(PAIRS)}
TRI = len(PAIRS)
TALL = TRI * SUB
LEFT = TALL // 3
RIGHT = TALL // 2
STEP = 224


def swapped(block, axis, apart):
    count = lax.axis_size(axis)
    route = []
    for low in range(count):
        high = low | 1 << apart
        if high != low and high < count:
            route += [(low, high), (high, low)]
    return lax.ppermute(block, axis, route)


def general(gradient):
    rows_dev, cols_dev = gradient.shape
    col_blocks = cols_dev // BLOCK
    share_count = BLOCK // rows_dev
    sections = share_count.bit_length() - 1
    row_count = lax.axis_size("row")
    row_index = lax.axis_index("row")
    row_blocks = M // BLOCK
    my_block = row_index // share_count
    offset = row_index % share_count * rows_dev
    slots = (jnp.arange(row_blocks) == my_block).astype(jnp.float32)
    band = gradient
    for bit in range(sections):
        partner = swapped(band, "row", bit)
        upper = row_index // 2**bit % 2 == 1
        band = jnp.where(
            upper, jnp.concatenate([partner, band], 0), jnp.concatenate([band, partner], 0)
        )
    grad_three = gradient.reshape(rows_dev, col_blocks, BLOCK)
    grad_wide = grad_three.astype(jnp.float32)
    grad_tiles = jnp.sum(grad_wide * grad_wide, axis=(0, 2))
    grad_slots = slots[:, None] * grad_tiles[None, :]
    grad_total = lax.psum(grad_slots, "row")
    left_part = lax.dot_general(
        gradient, band, (((1,), (1,)), ((), ())), preferred_element_type=jnp.float32
    )
    row_place = offset + lax.broadcasted_iota(jnp.int32, (rows_dev, 1), 0)
    left_rows = lax.psum(left_part, "col")
    diagonal = (lax.broadcasted_iota(jnp.int32, (rows_dev, BLOCK), 1) == row_place).astype(
        jnp.float32
    )
    left_rows = left_rows + damping * diagonal
    left_total = lax.psum(slots * jnp.sum(left_rows * left_rows), "row")
    left_scale = jnp.sqrt(jnp.sum(left_total * slots))
    left_root = ((5.0 * diagonal - left_rows / left_scale) * 0.25 * left_scale ** (-0.25)).astype(
        jnp.bfloat16
    )
    right_rows = BLOCK // row_count
    portion = grad_three
    right_share = lax.psum_scatter(
        jnp.einsum("rjc,rjd->cjd", portion, grad_three, preferred_element_type=jnp.float32),
        "row",
        scatter_dimension=0,
        tiled=True,
    )
    right_place = row_index * right_rows + lax.broadcasted_iota(
        jnp.int32, (right_rows, 1, BLOCK), 0
    )
    right_diagonal = (
        lax.broadcasted_iota(jnp.int32, (right_rows, 1, BLOCK), 2) == right_place
    ).astype(jnp.float32)
    right_share = right_share + damping * right_diagonal
    right_squares = jnp.sum(right_share * right_share, axis=(0, 2))
    right_total = lax.psum(right_squares, "row")
    right_scale = jnp.sqrt(right_total)[None, :, None]
    right_piece = (
        (5.0 * right_diagonal - right_share / right_scale) * 0.25 * right_scale ** (-0.25)
    ).astype(jnp.bfloat16)
    portion = grad_three
    projected = jnp.einsum(
        "rjc,cjd->rjd",
        portion,
        lax.all_gather(right_piece, "row", axis=0, tiled=True),
        preferred_element_type=jnp.float32,
    ).astype(jnp.bfloat16)
    projected_band = projected
    for bit in range(sections):
        partner_rows = swapped(projected_band, "row", bit)
        upper = row_index // 2**bit % 2 == 1
        projected_band = jnp.where(
            upper,
            jnp.concatenate([partner_rows, projected_band], 0),
            jnp.concatenate([projected_band, partner_rows], 0),
        )
    precond = jnp.einsum(
        "rk,kjd->rjd", left_root, projected_band, preferred_element_type=jnp.float32
    )
    pre_tiles = jnp.sum(precond * precond, axis=(0, 2))
    update_total = lax.psum(slots[:, None] * pre_tiles[None, :], "row")
    grad_mine = jnp.sum(grad_total * slots[:, None], axis=0)
    update_mine = jnp.sum(update_total * slots[:, None], axis=0)
    factor = jnp.sqrt(grad_mine) / jnp.sqrt(update_mine + 1e-06)
    return (precond * factor[None, :, None]).astype(jnp.bfloat16).reshape(rows_dev, cols_dev)


def eye():
    shape = (SUB, SUB)
    return lax.broadcasted_iota(jnp.int32, shape, 0) == lax.broadcasted_iota(jnp.int32, shape, 1)


def add_into(dst, dst_at, one, one_at, two, two_at, rows):
    def piece(m, carry):
        def part(ref, at):
            return ref.at[pl.ds(pl.multiple_of(at + m * STEP, 16), STEP), :]

        part(dst, dst_at)[...] = (
            part(one, one_at)[...].astype(jnp.float32) + part(two, two_at)[...].astype(jnp.float32)
        ).astype(jnp.bfloat16)
        return carry

    lax.fori_loop(0, rows // STEP, piece, 0)


def gram_kernel(
    g_ref,
    left_out,
    left_diag_out,
    right_out,
    right_diag_out,
    left_part,
    left_sum,
    left_y,
    left_near,
    left_far,
    right_part,
    right_sum,
    right_core,
    right_x,
    left_diag,
    left_diag_in,
    right_diag,
    right_diag_in,
    send_sem,
    recv_sem,
    out_sem,
):
    row = lax.axis_index("row")
    col = lax.axis_index("col")

    def flipped(index, apart):
        bit = lax.rem(index // apart, 2)
        return bit, index + apart - 2 * apart * bit

    y_bit, y_mate = flipped(col, 1)
    near_bit, near_mate = flipped(col, 2)
    far_bit, far_mate = flipped(col, 4)
    core_bit, core_mate = flipped(row, 1)
    _, x_mate = flipped(row, 2)
    to_y, to_near, to_far = {"col": y_mate}, {"col": near_mate}, {"col": far_mate}
    to_core, to_x = {"row": core_mate}, {"row": x_mate}

    barrier = pltpu.get_barrier_semaphore()
    mates = (to_y, to_near, to_far, to_core, to_x)
    for mate in mates:
        pl.semaphore_signal(barrier, inc=1, device_id=mate, device_id_type=pl.DeviceIdType.MESH)

    copies = {}

    def send(name, src, dst, mate):
        index = len(copies)
        copy = pltpu.make_async_remote_copy(
            src_ref=src,
            dst_ref=dst,
            send_sem=send_sem.at[index],
            recv_sem=recv_sem.at[index],
            device_id=mate,
            device_id_type=pl.DeviceIdType.MESH,
        )
        copy.start()
        copies[name] = copy

    def got(name):
        copies[name].wait_recv()

    outs = []

    def emit(src, dst):
        copy = pltpu.make_async_copy(src, dst, out_sem.at[len(outs)])
        copy.start()
        outs.append(copy)

    def rows(ref, at, count):
        return ref.at[pl.ds(pl.multiple_of(at, 16), count), :]

    def store_strip(a, strip, part, base, diag, diag_base):
        for b in range(a, STRIPS):
            block = strip[:, (b - a) * SUB : (b - a + 1) * SUB]
            if a == b:
                diag[:, diag_base + a * SUB : diag_base + (a + 1) * SUB] = jnp.sum(
                    jnp.where(eye(), block, 0.0), axis=0, keepdims=True
                )
            at = base + SLOT[a, b] * SUB
            part[at : at + SUB, :] = block.astype(jnp.bfloat16)

    def left_strip(a):
        strip = lax.dot_general(
            g_ref[a * SUB : (a + 1) * SUB, :],
            g_ref[a * SUB :, :],
            (((1,), (1,)), ((), ())),
            preferred_element_type=jnp.float32,
        )
        store_strip(a, strip, left_part, 0, left_diag.at[0], 0)

    def right_strip(j, a):
        low, high = j * BLOCK + a * SUB, (j + 1) * BLOCK
        strip = lax.dot_general(
            g_ref[:, low : low + SUB],
            g_ref[:, low:high],
            (((0,), (0,)), ((), ())),
            preferred_element_type=jnp.float32,
        )
        store_strip(a, strip, right_part, j * TALL, right_diag.at[0], j * BLOCK)

    half, quarter, eighth = LEFT // 2, LEFT // 4, LEFT // 8

    def at_y(c):
        return c * LEFT + y_bit * half

    def at_near(c):
        return at_y(c) + near_bit * quarter

    def at_far(c):
        return at_near(c) + far_bit * eighth

    def y_send(c):
        send(("y", c), rows(left_part, c * LEFT + (1 - y_bit) * half, half),
             rows(left_y, c * half, half), to_y)

    def near_send(c):
        got(("y", c))
        add_into(left_part, at_y(c), left_part, at_y(c), left_y, c * half, half)
        send(("near", c), rows(left_part, at_y(c) + (1 - near_bit) * quarter, quarter),
             rows(left_near, c * quarter, quarter), to_near)

    def far_send(c):
        got(("near", c))
        add_into(left_part, at_near(c), left_part, at_near(c), left_near, c * quarter, quarter)
        send(("far", c), rows(left_part, at_near(c) + (1 - far_bit) * eighth, eighth),
             rows(left_far, c * eighth, eighth), to_far)

    def far_back(c):
        got(("far", c))
        add_into(left_sum, at_far(c), left_part, at_far(c), left_far, c * eighth, eighth)
        mine = rows(left_sum, at_far(c), eighth)
        send(("far_back", c), mine, mine, to_far)

    def near_back(c):
        got(("far_back", c))
        mine = rows(left_sum, at_near(c), quarter)
        send(("near_back", c), mine, mine, to_near)

    def y_back(c):
        got(("near_back", c))
        mine = rows(left_sum, at_y(c), half)
        send(("y_back", c), mine, mine, to_y)

    def left_done(c):
        got(("y_back", c))
        emit(rows(left_sum, c * LEFT, LEFT), rows(left_out, c * LEFT, LEFT))

    share = RIGHT // 2

    def at_core(k):
        return k * RIGHT + core_bit * share

    def core_send(k):
        send(("core", k), rows(right_part, k * RIGHT + (1 - core_bit) * share, share),
             rows(right_core, k * share, share), to_core)

    def x_send(k):
        got(("core", k))
        add_into(right_part, at_core(k), right_part, at_core(k), right_core, k * share, share)
        send(("x", k), rows(right_part, at_core(k), share), rows(right_x, k * share, share), to_x)

    def core_back(k):
        got(("x", k))
        add_into(right_sum, at_core(k), right_part, at_core(k), right_x, k * share, share)
        mine = rows(right_sum, at_core(k), share)
        send(("core_back", k), mine, mine, to_core)

    def right_done(k):
        got(("core_back", k))
        emit(rows(right_sum, k * RIGHT, RIGHT), rows(right_out, k * RIGHT, RIGHT))

    def diag_send(name, slot, own, landing, mate):
        send(("diag", name), own.at[slot], landing.at[slot], mate)

    def diag_add(name, slot, own, landing):
        got(("diag", name))
        own[slot + 1] = own[slot] + landing[slot]

    left_strip(0)
    left_strip(1)
    pl.semaphore_wait(barrier, len(mates))
    y_send(0)
    left_strip(2)
    y_send(1)
    for a in range(3, STRIPS):
        left_strip(a)
    y_send(2)
    diag_send("y", 0, left_diag, left_diag_in, to_y)
    right_strip(0, 0)
    right_strip(0, 1)
    core_send(0)
    near_send(0)
    for a in range(2, STRIPS):
        right_strip(0, a)
    core_send(1)
    x_send(0)
    far_send(0)
    right_strip(1, 0)
    right_strip(1, 1)
    core_send(2)
    x_send(1)
    near_send(1)
    for a in range(2, STRIPS):
        right_strip(1, a)
    core_send(3)
    diag_send("core", 0, right_diag, right_diag_in, to_core)
    x_send(2)
    x_send(3)
    far_back(0)
    diag_add("y", 0, left_diag, left_diag_in)
    diag_send("near", 1, left_diag, left_diag_in, to_near)
    diag_add("core", 0, right_diag, right_diag_in)
    diag_send("x", 1, right_diag, right_diag_in, to_x)
    far_send(1)
    near_back(0)
    near_send(2)
    diag_add("near", 1, left_diag, left_diag_in)
    diag_send("far", 2, left_diag, left_diag_in, to_far)
    far_back(1)
    y_back(0)
    far_send(2)
    core_back(0)
    near_back(1)
    far_back(2)
    y_back(1)
    near_back(2)
    diag_add("x", 1, right_diag, right_diag_in)
    diag_add("far", 2, left_diag, left_diag_in)
    left_diag_out[...] = left_diag[3]
    right_diag_out[...] = right_diag[2]
    core_back(1)
    left_done(0)
    y_back(2)
    right_done(0)
    left_done(1)
    core_back(2)
    right_done(1)
    left_done(2)
    core_back(3)
    right_done(2)
    right_done(3)
    for copy in copies.values():
        copy.wait_send()
    for copy in outs:
        copy.wait()


def build_root(tri_ref, diag_ref, root_ref):
    diag = diag_ref[...] + damping
    total = jnp.sum(diag * diag, axis=1, keepdims=True)
    squares = jnp.zeros((SUB, SUB), jnp.float32)
    for a, b in PAIRS:
        block = tri_ref[SLOT[a, b] * SUB : (SLOT[a, b] + 1) * SUB, :].astype(jnp.float32)
        if a == b:
            block = jnp.where(eye(), 0.0, block)
            squares = squares + block * block
        else:
            squares = squares + 2.0 * (block * block)
    squares = jnp.sum(jnp.sum(squares, axis=0, keepdims=True), axis=1, keepdims=True)
    scale = jnp.sqrt(total + squares)
    inverse = 1.0 / scale
    gain = 0.25 / jnp.sqrt(jnp.sqrt(scale))
    on_diag = (5.0 - diag * inverse) * gain
    for a, b in PAIRS:
        block = (0.0 - tri_ref[SLOT[a, b] * SUB : (SLOT[a, b] + 1) * SUB, :].astype(jnp.float32) * inverse) * gain
        rows, cols = slice(a * SUB, (a + 1) * SUB), slice(b * SUB, (b + 1) * SUB)
        if a == b:
            block = jnp.where(eye(), on_diag[:, cols], block)
        else:
            root_ref[cols, rows] = block.T.astype(jnp.bfloat16)
        root_ref[rows, cols] = block.astype(jnp.bfloat16)


CHUNK = 512


def apply_kernel(
    g_ref, left_ref, left_diag, right_ref, right_diag, out_ref, left_root, right_root, proj, pre
):
    @pl.when(pl.program_id(0) == 0)
    def _():
        build_root(left_ref, left_diag, left_root)

    build_root(right_ref, right_diag, right_root)
    zero = jnp.zeros((8, CHUNK), jnp.float32)

    def sums(wide):
        return jnp.sum((wide * wide).reshape(-1, 8, CHUNK), axis=0)

    def step(n, carry):
        grad_sum, pre_sum = carry
        cols = pl.ds(pl.multiple_of(n * CHUNK, CHUNK), CHUNK)
        proj[...] = jnp.dot(
            g_ref[...], right_root[:, cols], preferred_element_type=jnp.float32
        ).astype(jnp.bfloat16)
        block = jnp.dot(left_root[...], proj[...], preferred_element_type=jnp.float32)
        pre[:, cols] = block
        return grad_sum + sums(g_ref[:, cols].astype(jnp.float32)), pre_sum + sums(block)

    grad_sum, pre_sum = lax.fori_loop(0, BLOCK // CHUNK, step, (zero, zero))

    def whole(part):
        return jnp.sum(jnp.sum(part, axis=0, keepdims=True), axis=1, keepdims=True)

    factor = jnp.sqrt(whole(grad_sum)) / jnp.sqrt(whole(pre_sum) + 1e-06)

    def scale_rows(m, carry):
        rows = pl.ds(pl.multiple_of(m * SUB, SUB), SUB)
        out_ref[rows, :] = (pre[rows, :] * factor).astype(jnp.bfloat16)
        return carry

    lax.fori_loop(0, STRIPS, scale_rows, 0)


VMEM_LIMIT = 60 * 1024 * 1024


def local(gradient):
    rows_dev, cols_dev = gradient.shape
    if (rows_dev, cols_dev) != (BLOCK, 2 * BLOCK) or (
        (lax.axis_size("row"), lax.axis_size("col")) != (4, 8)
    ):
        return general(gradient)
    col_blocks = cols_dev // BLOCK
    params = pltpu.CompilerParams(vmem_limit_bytes=VMEM_LIMIT)
    vmem = pl.BlockSpec(memory_space=pltpu.VMEM)
    anywhere = pl.BlockSpec(memory_space=pl.ANY)
    half = jnp.bfloat16
    left_tri, left_diag, right_tri, right_diag = pl.pallas_call(
        gram_kernel,
        in_specs=[vmem],
        out_specs=(anywhere, vmem, anywhere, vmem),
        out_shape=(
            jax.ShapeDtypeStruct((TALL, SUB), half),
            jax.ShapeDtypeStruct((1, BLOCK), jnp.float32),
            jax.ShapeDtypeStruct((col_blocks * TALL, SUB), half),
            jax.ShapeDtypeStruct((1, cols_dev), jnp.float32),
        ),
        scratch_shapes=[
            pltpu.VMEM((TALL, SUB), half),
            pltpu.VMEM((TALL, SUB), half),
            pltpu.VMEM((TALL // 2, SUB), half),
            pltpu.VMEM((TALL // 4, SUB), half),
            pltpu.VMEM((TALL // 8, SUB), half),
            pltpu.VMEM((col_blocks * TALL, SUB), half),
            pltpu.VMEM((col_blocks * TALL, SUB), half),
            pltpu.VMEM((col_blocks * TALL // 2, SUB), half),
            pltpu.VMEM((col_blocks * TALL // 2, SUB), half),
            pltpu.VMEM((4, 1, BLOCK), jnp.float32),
            pltpu.VMEM((3, 1, BLOCK), jnp.float32),
            pltpu.VMEM((3, 1, cols_dev), jnp.float32),
            pltpu.VMEM((2, 1, cols_dev), jnp.float32),
            pltpu.SemaphoreType.DMA((35,)),
            pltpu.SemaphoreType.DMA((35,)),
            pltpu.SemaphoreType.DMA((7,)),
        ],
        compiler_params=pltpu.CompilerParams(
            vmem_limit_bytes=VMEM_LIMIT, collective_id=0, has_side_effects=True
        ),
    )(gradient)
    return pl.pallas_call(
        apply_kernel,
        grid=(col_blocks,),
        in_specs=[
            pl.BlockSpec((BLOCK, BLOCK), lambda j: (0, j)),
            pl.BlockSpec((TALL, SUB), lambda j: (0, 0)),
            pl.BlockSpec((1, BLOCK), lambda j: (0, 0)),
            pl.BlockSpec((TALL, SUB), lambda j: (j, 0)),
            pl.BlockSpec((1, BLOCK), lambda j: (0, j)),
        ],
        out_specs=pl.BlockSpec((BLOCK, BLOCK), lambda j: (0, j)),
        out_shape=jax.ShapeDtypeStruct((BLOCK, cols_dev), jnp.bfloat16),
        scratch_shapes=[
            pltpu.VMEM((BLOCK, BLOCK), jnp.bfloat16),
            pltpu.VMEM((BLOCK, BLOCK), jnp.bfloat16),
            pltpu.VMEM((BLOCK, CHUNK), jnp.bfloat16),
            pltpu.VMEM((BLOCK, BLOCK), jnp.float32),
        ],
        compiler_params=params,
    )(gradient, left_tri, left_diag, right_tri, right_diag)


def solution(mesh):
    in_specs = (P("row", "col"),)
    out_specs = P("row", "col")
    return jax.shard_map(local, mesh=mesh, in_specs=in_specs, out_specs=out_specs, check_vma=False)
```

```python
import jax
import jax.numpy as jnp
from jax import lax
from jax.experimental import pallas as pl
from jax.experimental.pallas import tpu as pltpu
from jax.sharding import PartitionSpec as P

M = 6144
BLOCK = 1536
SUB = 256


damping = 0.001

STRIPS = BLOCK // SUB
PAIRS = [(a, b) for a in range(STRIPS) for b in range(a, STRIPS)]
SLOT = {pair: index for index, pair in enumerate(PAIRS)}
TRI = len(PAIRS)
TALL = TRI * SUB
LEFT = TALL // 3
RIGHT = TALL // 2
STEP = 224


def swapped(block, axis, apart):
    count = lax.axis_size(axis)
    route = []
    for low in range(count):
        high = low | 1 << apart
        if high != low and high < count:
            route += [(low, high), (high, low)]
    return lax.ppermute(block, axis, route)


def general(gradient):
    rows_dev, cols_dev = gradient.shape
    col_blocks = cols_dev // BLOCK
    share_count = BLOCK // rows_dev
    sections = share_count.bit_length() - 1
    row_count = lax.axis_size("row")
    row_index = lax.axis_index("row")
    row_blocks = M // BLOCK
    my_block = row_index // share_count
    offset = row_index % share_count * rows_dev
    slots = (jnp.arange(row_blocks) == my_block).astype(jnp.float32)
    band = gradient
    for bit in range(sections):
        partner = swapped(band, "row", bit)
        upper = row_index // 2**bit % 2 == 1
        band = jnp.where(
            upper, jnp.concatenate([partner, band], 0), jnp.concatenate([band, partner], 0)
        )
    grad_three = gradient.reshape(rows_dev, col_blocks, BLOCK)
    grad_wide = grad_three.astype(jnp.float32)
    grad_tiles = jnp.sum(grad_wide * grad_wide, axis=(0, 2))
    grad_slots = slots[:, None] * grad_tiles[None, :]
    grad_total = lax.psum(grad_slots, "row")
    left_part = lax.dot_general(
        gradient, band, (((1,), (1,)), ((), ())), preferred_element_type=jnp.float32
    )
    row_place = offset + lax.broadcasted_iota(jnp.int32, (rows_dev, 1), 0)
    left_rows = lax.psum(left_part, "col")
    diagonal = (lax.broadcasted_iota(jnp.int32, (rows_dev, BLOCK), 1) == row_place).astype(
        jnp.float32
    )
    left_rows = left_rows + damping * diagonal
    left_total = lax.psum(slots * jnp.sum(left_rows * left_rows), "row")
    left_scale = jnp.sqrt(jnp.sum(left_total * slots))
    left_root = ((5.0 * diagonal - left_rows / left_scale) * 0.25 * left_scale ** (-0.25)).astype(
        jnp.bfloat16
    )
    right_rows = BLOCK // row_count
    portion = grad_three
    right_share = lax.psum_scatter(
        jnp.einsum("rjc,rjd->cjd", portion, grad_three, preferred_element_type=jnp.float32),
        "row",
        scatter_dimension=0,
        tiled=True,
    )
    right_place = row_index * right_rows + lax.broadcasted_iota(
        jnp.int32, (right_rows, 1, BLOCK), 0
    )
    right_diagonal = (
        lax.broadcasted_iota(jnp.int32, (right_rows, 1, BLOCK), 2) == right_place
    ).astype(jnp.float32)
    right_share = right_share + damping * right_diagonal
    right_squares = jnp.sum(right_share * right_share, axis=(0, 2))
    right_total = lax.psum(right_squares, "row")
    right_scale = jnp.sqrt(right_total)[None, :, None]
    right_piece = (
        (5.0 * right_diagonal - right_share / right_scale) * 0.25 * right_scale ** (-0.25)
    ).astype(jnp.bfloat16)
    portion = grad_three
    projected = jnp.einsum(
        "rjc,cjd->rjd",
        portion,
        lax.all_gather(right_piece, "row", axis=0, tiled=True),
        preferred_element_type=jnp.float32,
    ).astype(jnp.bfloat16)
    projected_band = projected
    for bit in range(sections):
        partner_rows = swapped(projected_band, "row", bit)
        upper = row_index // 2**bit % 2 == 1
        projected_band = jnp.where(
            upper,
            jnp.concatenate([partner_rows, projected_band], 0),
            jnp.concatenate([projected_band, partner_rows], 0),
        )
    precond = jnp.einsum(
        "rk,kjd->rjd", left_root, projected_band, preferred_element_type=jnp.float32
    )
    pre_tiles = jnp.sum(precond * precond, axis=(0, 2))
    update_total = lax.psum(slots[:, None] * pre_tiles[None, :], "row")
    grad_mine = jnp.sum(grad_total * slots[:, None], axis=0)
    update_mine = jnp.sum(update_total * slots[:, None], axis=0)
    factor = jnp.sqrt(grad_mine) / jnp.sqrt(update_mine + 1e-06)
    return (precond * factor[None, :, None]).astype(jnp.bfloat16).reshape(rows_dev, cols_dev)


def eye():
    shape = (SUB, SUB)
    return lax.broadcasted_iota(jnp.int32, shape, 0) == lax.broadcasted_iota(jnp.int32, shape, 1)


def add_into(dst, dst_at, one, one_at, two, two_at, rows):
    def piece(m, carry):
        def part(ref, at):
            return ref.at[pl.ds(pl.multiple_of(at + m * STEP, 16), STEP), :]

        part(dst, dst_at)[...] = (
            part(one, one_at)[...].astype(jnp.float32) + part(two, two_at)[...].astype(jnp.float32)
        ).astype(jnp.bfloat16)
        return carry

    lax.fori_loop(0, rows // STEP, piece, 0)


def build_root(tri_ref, diag_ref, root_ref):
    diag = diag_ref[...] + damping
    total = jnp.sum(diag * diag, axis=1, keepdims=True)
    squares = jnp.zeros((SUB, SUB), jnp.float32)
    for a, b in PAIRS:
        block = tri_ref[SLOT[a, b] * SUB : (SLOT[a, b] + 1) * SUB, :].astype(jnp.float32)
        if a == b:
            block = jnp.where(eye(), 0.0, block)
            squares = squares + block * block
        else:
            squares = squares + 2.0 * (block * block)
    squares = jnp.sum(jnp.sum(squares, axis=0, keepdims=True), axis=1, keepdims=True)
    scale = jnp.sqrt(total + squares)
    inverse = 1.0 / scale
    gain = 0.25 / jnp.sqrt(jnp.sqrt(scale))
    on_diag = (5.0 - diag * inverse) * gain
    for a, b in PAIRS:
        block = (0.0 - tri_ref[SLOT[a, b] * SUB : (SLOT[a, b] + 1) * SUB, :].astype(jnp.float32) * inverse) * gain
        rows, cols = slice(a * SUB, (a + 1) * SUB), slice(b * SUB, (b + 1) * SUB)
        if a == b:
            block = jnp.where(eye(), on_diag[:, cols], block)
        else:
            root_ref[cols, rows] = block.T.astype(jnp.bfloat16)
        root_ref[rows, cols] = block.astype(jnp.bfloat16)


CHUNK = 512


def gram_kernel(
    g_ref,
    left_out,
    left_diag_out,
    grad_out,
    proj_out,
    left_part,
    left_sum,
    left_y,
    left_near,
    left_far,
    right_part,
    right_sum,
    right_core,
    right_x,
    left_diag,
    left_diag_in,
    right_diag,
    right_diag_in,
    right_root,
    proj,
    send_sem,
    recv_sem,
    out_sem,
):
    row = lax.axis_index("row")
    col = lax.axis_index("col")

    def flipped(index, apart):
        bit = lax.rem(index // apart, 2)
        return bit, index + apart - 2 * apart * bit

    y_bit, y_mate = flipped(col, 1)
    near_bit, near_mate = flipped(col, 2)
    far_bit, far_mate = flipped(col, 4)
    core_bit, core_mate = flipped(row, 1)
    _, x_mate = flipped(row, 2)
    to_y, to_near, to_far = {"col": y_mate}, {"col": near_mate}, {"col": far_mate}
    to_core, to_x = {"row": core_mate}, {"row": x_mate}

    barrier = pltpu.get_barrier_semaphore()
    mates = (to_y, to_near, to_far, to_core, to_x)
    for mate in mates:
        pl.semaphore_signal(barrier, inc=1, device_id=mate, device_id_type=pl.DeviceIdType.MESH)

    copies = {}

    def send(name, src, dst, mate):
        index = len(copies)
        copy = pltpu.make_async_remote_copy(
            src_ref=src,
            dst_ref=dst,
            send_sem=send_sem.at[index],
            recv_sem=recv_sem.at[index],
            device_id=mate,
            device_id_type=pl.DeviceIdType.MESH,
        )
        copy.start()
        copies[name] = copy

    def got(name):
        copies[name].wait_recv()

    outs = []

    def emit(src, dst):
        copy = pltpu.make_async_copy(src, dst, out_sem.at[len(outs)])
        copy.start()
        outs.append(copy)

    def rows(ref, at, count):
        return ref.at[pl.ds(pl.multiple_of(at, 16), count), :]

    def store_strip(a, strip, part, base, diag, diag_base):
        for b in range(a, STRIPS):
            block = strip[:, (b - a) * SUB : (b - a + 1) * SUB]
            if a == b:
                diag[:, diag_base + a * SUB : diag_base + (a + 1) * SUB] = jnp.sum(
                    jnp.where(eye(), block, 0.0), axis=0, keepdims=True
                )
            at = base + SLOT[a, b] * SUB
            part[at : at + SUB, :] = block.astype(jnp.bfloat16)

    def left_strip(a):
        strip = lax.dot_general(
            g_ref[a * SUB : (a + 1) * SUB, :],
            g_ref[a * SUB :, :],
            (((1,), (1,)), ((), ())),
            preferred_element_type=jnp.float32,
        )
        store_strip(a, strip, left_part, 0, left_diag.at[0], 0)

    def right_strip(j, a):
        low, high = j * BLOCK + a * SUB, (j + 1) * BLOCK
        strip = lax.dot_general(
            g_ref[:, low : low + SUB],
            g_ref[:, low:high],
            (((0,), (0,)), ((), ())),
            preferred_element_type=jnp.float32,
        )
        store_strip(a, strip, right_part, j * TALL, right_diag.at[0], j * BLOCK)

    half, quarter, eighth = LEFT // 2, LEFT // 4, LEFT // 8

    def at_y(c):
        return c * LEFT + y_bit * half

    def at_near(c):
        return at_y(c) + near_bit * quarter

    def at_far(c):
        return at_near(c) + far_bit * eighth

    def y_send(c):
        send(("y", c), rows(left_part, c * LEFT + (1 - y_bit) * half, half),
             rows(left_y, c * half, half), to_y)

    def near_send(c):
        got(("y", c))
        add_into(left_part, at_y(c), left_part, at_y(c), left_y, c * half, half)
        send(("near", c), rows(left_part, at_y(c) + (1 - near_bit) * quarter, quarter),
             rows(left_near, c * quarter, quarter), to_near)

    def far_send(c):
        got(("near", c))
        add_into(left_part, at_near(c), left_part, at_near(c), left_near, c * quarter, quarter)
        send(("far", c), rows(left_part, at_near(c) + (1 - far_bit) * eighth, eighth),
             rows(left_far, c * eighth, eighth), to_far)

    def far_back(c):
        got(("far", c))
        add_into(left_sum, at_far(c), left_part, at_far(c), left_far, c * eighth, eighth)
        mine = rows(left_sum, at_far(c), eighth)
        send(("far_back", c), mine, mine, to_far)

    def near_back(c):
        got(("far_back", c))
        mine = rows(left_sum, at_near(c), quarter)
        send(("near_back", c), mine, mine, to_near)

    def y_back(c):
        got(("near_back", c))
        mine = rows(left_sum, at_y(c), half)
        send(("y_back", c), mine, mine, to_y)

    def left_done(c):
        got(("y_back", c))
        emit(rows(left_sum, c * LEFT, LEFT), rows(left_out, c * LEFT, LEFT))

    share = RIGHT // 2

    def at_core(k):
        return k * RIGHT + core_bit * share

    def core_send(k):
        send(("core", k), rows(right_part, k * RIGHT + (1 - core_bit) * share, share),
             rows(right_core, k * share, share), to_core)

    def x_send(k):
        got(("core", k))
        add_into(right_part, at_core(k), right_part, at_core(k), right_core, k * share, share)
        send(("x", k), rows(right_part, at_core(k), share), rows(right_x, k * share, share), to_x)

    def core_back(k):
        got(("x", k))
        add_into(right_sum, at_core(k), right_part, at_core(k), right_x, k * share, share)
        mine = rows(right_sum, at_core(k), share)
        send(("core_back", k), mine, mine, to_core)

    def diag_send(name, slot, own, landing, mate):
        send(("diag", name), own.at[slot], landing.at[slot], mate)

    def diag_add(name, slot, own, landing):
        got(("diag", name))
        own[slot + 1] = own[slot] + landing[slot]

    def project(j, n):
        low = j * BLOCK + n * CHUNK
        proj[:, low : low + CHUNK] = jnp.dot(
            g_ref[:, j * BLOCK : (j + 1) * BLOCK],
            right_root[:, n * CHUNK : (n + 1) * CHUNK],
            preferred_element_type=jnp.float32,
        ).astype(jnp.bfloat16)

    def right_ready(j):
        got(("core_back", 2 * j))
        got(("core_back", 2 * j + 1))
        build_root(
            right_sum.at[j * TALL : (j + 1) * TALL, :],
            right_diag.at[2, :, j * BLOCK : (j + 1) * BLOCK],
            right_root,
        )

    def emit_proj(j):
        cols = slice(j * BLOCK, (j + 1) * BLOCK)
        emit(proj.at[:, cols], proj_out.at[:, cols])

    right_strip(0, 0)
    right_strip(0, 1)
    pl.semaphore_wait(barrier, len(mates))
    core_send(0)
    left_strip(0)
    x_send(0)
    left_strip(1)
    y_send(0)
    for a in range(2, STRIPS):
        right_strip(0, a)
    core_send(1)
    left_strip(2)
    y_send(1)
    x_send(1)
    for a in range(3, STRIPS):
        left_strip(a)
    y_send(2)
    diag_send("y", 0, left_diag, left_diag_in, to_y)
    near_send(0)
    right_strip(1, 0)
    right_strip(1, 1)
    core_send(2)
    for a in range(2, STRIPS):
        right_strip(1, a)
    core_send(3)
    diag_send("core", 0, right_diag, right_diag_in, to_core)
    grad_out[...] = right_diag[0]
    far_send(0)
    x_send(2)
    core_back(0)
    near_send(1)
    x_send(3)
    diag_add("y", 0, left_diag, left_diag_in)
    diag_send("near", 1, left_diag, left_diag_in, to_near)
    diag_add("core", 0, right_diag, right_diag_in)
    diag_send("x", 1, right_diag, right_diag_in, to_x)
    far_back(0)
    far_send(1)
    core_back(1)
    diag_add("x", 1, right_diag, right_diag_in)
    diag_add("near", 1, left_diag, left_diag_in)
    diag_send("far", 2, left_diag, left_diag_in, to_far)
    near_back(0)
    near_send(2)
    right_ready(0)
    far_back(1)
    y_back(0)
    far_send(2)
    project(0, 0)
    near_back(1)
    project(0, 1)
    far_back(2)
    y_back(1)
    core_back(2)
    project(0, 2)
    emit_proj(0)
    near_back(2)
    diag_add("far", 2, left_diag, left_diag_in)
    left_diag_out[...] = left_diag[3]
    left_done(0)
    y_back(2)
    core_back(3)
    left_done(1)
    right_ready(1)
    project(1, 0)
    left_done(2)
    project(1, 1)
    project(1, 2)
    emit_proj(1)
    for copy in copies.values():
        copy.wait_send()
    for copy in outs:
        copy.wait()


def apply_kernel(proj_ref, grad_ref, left_ref, left_diag, out_ref, left_root, pre):
    @pl.when(pl.program_id(0) == 0)
    def _():
        build_root(left_ref, left_diag, left_root)

    def step(n, pre_sum):
        cols = pl.ds(pl.multiple_of(n * CHUNK, CHUNK), CHUNK)
        block = jnp.dot(left_root[...], proj_ref[:, cols], preferred_element_type=jnp.float32)
        pre[:, cols] = block
        return pre_sum + jnp.sum((block * block).reshape(-1, 8, CHUNK), axis=0)

    pre_sum = lax.fori_loop(0, BLOCK // CHUNK, step, jnp.zeros((8, CHUNK), jnp.float32))
    pre_sum = jnp.sum(jnp.sum(pre_sum, axis=0, keepdims=True), axis=1, keepdims=True)
    grad_sum = jnp.sum(grad_ref[...], axis=1, keepdims=True)
    factor = jnp.sqrt(grad_sum) / jnp.sqrt(pre_sum + 1e-06)

    def scale_rows(m, carry):
        rows = pl.ds(pl.multiple_of(m * SUB, SUB), SUB)
        out_ref[rows, :] = (pre[rows, :] * factor).astype(jnp.bfloat16)
        return carry

    lax.fori_loop(0, STRIPS, scale_rows, 0)


VMEM_LIMIT = 60 * 1024 * 1024


def local(gradient):
    rows_dev, cols_dev = gradient.shape
    if (rows_dev, cols_dev) != (BLOCK, 2 * BLOCK) or (
        (lax.axis_size("row"), lax.axis_size("col")) != (4, 8)
    ):
        return general(gradient)
    col_blocks = cols_dev // BLOCK
    params = pltpu.CompilerParams(vmem_limit_bytes=VMEM_LIMIT)
    vmem = pl.BlockSpec(memory_space=pltpu.VMEM)
    anywhere = pl.BlockSpec(memory_space=pl.ANY)
    half = jnp.bfloat16
    left_tri, left_diag, grad_diag, proj = pl.pallas_call(
        gram_kernel,
        in_specs=[vmem],
        out_specs=(anywhere, vmem, vmem, anywhere),
        out_shape=(
            jax.ShapeDtypeStruct((TALL, SUB), half),
            jax.ShapeDtypeStruct((1, BLOCK), jnp.float32),
            jax.ShapeDtypeStruct((1, cols_dev), jnp.float32),
            jax.ShapeDtypeStruct((BLOCK, cols_dev), half),
        ),
        scratch_shapes=[
            pltpu.VMEM((TALL, SUB), half),
            pltpu.VMEM((TALL, SUB), half),
            pltpu.VMEM((TALL // 2, SUB), half),
            pltpu.VMEM((TALL // 4, SUB), half),
            pltpu.VMEM((TALL // 8, SUB), half),
            pltpu.VMEM((col_blocks * TALL, SUB), half),
            pltpu.VMEM((col_blocks * TALL, SUB), half),
            pltpu.VMEM((col_blocks * TALL // 2, SUB), half),
            pltpu.VMEM((col_blocks * TALL // 2, SUB), half),
            pltpu.VMEM((4, 1, BLOCK), jnp.float32),
            pltpu.VMEM((3, 1, BLOCK), jnp.float32),
            pltpu.VMEM((3, 1, cols_dev), jnp.float32),
            pltpu.VMEM((2, 1, cols_dev), jnp.float32),
            pltpu.VMEM((BLOCK, BLOCK), half),
            pltpu.VMEM((BLOCK, cols_dev), half),
            pltpu.SemaphoreType.DMA((35,)),
            pltpu.SemaphoreType.DMA((35,)),
            pltpu.SemaphoreType.DMA((5,)),
        ],
        compiler_params=pltpu.CompilerParams(
            vmem_limit_bytes=VMEM_LIMIT, collective_id=0, has_side_effects=True
        ),
    )(gradient)
    return pl.pallas_call(
        apply_kernel,
        grid=(col_blocks,),
        in_specs=[
            pl.BlockSpec((BLOCK, BLOCK), lambda j: (0, j)),
            pl.BlockSpec((1, BLOCK), lambda j: (0, j)),
            pl.BlockSpec((TALL, SUB), lambda j: (0, 0)),
            pl.BlockSpec((1, BLOCK), lambda j: (0, 0)),
        ],
        out_specs=pl.BlockSpec((BLOCK, BLOCK), lambda j: (0, j)),
        out_shape=jax.ShapeDtypeStruct((BLOCK, cols_dev), jnp.bfloat16),
        scratch_shapes=[
            pltpu.VMEM((BLOCK, BLOCK), jnp.bfloat16),
            pltpu.VMEM((BLOCK, BLOCK), jnp.float32),
        ],
        compiler_params=params,
    )(proj, grad_diag, left_tri, left_diag)


def solution(mesh):
    in_specs = (P("row", "col"),)
    out_specs = P("row", "col")
    return jax.shard_map(local, mesh=mesh, in_specs=in_specs, out_specs=out_specs, check_vma=False)
```
